256 devices in a mesh: rep: 16 (over y, x_lo, core), fsdp: 16 (over z, x_hi).
Axes of the slice: x: 4 (x_hi: 2, x_lo: 2; x = x_hi * 2 + x_lo), y: 4, z: 8, core: 2. Of those that a mesh axis runs over, the one named last changes fastest.
Arguments:
- hidden: bfloat16 [16, 8192, 8192], P('rep', 'fsdp'), may hold values from -6 to 6
- own_weight: bfloat16 [16, 8192, 512], P('rep', 'fsdp'), may hold values from -0.0625 to 0.0625
- stale_weight: bfloat16 [16, 8192, 512], P('rep', 'fsdp'), may hold values from -0.0625 to 0.0625
- token_ids: int32 [16, 8192], P('rep', 'fsdp'), may hold values from 0 to 128255, as said below
- matching: int32 [16], replicated, may hold values from 0 to 15, as said below
Outputs:
- gradient: float32 [16, 8192, 512], P('rep', 'fsdp')
The draws below stay inside these ranges and needn't reach their ends.
Inputs may be any that keep to these rules, and one draw needn't show every extreme that they name: `token_ids`: 0 marks padding; every block of 512 consecutive positions of a group begins with a nonzero id. matching[r] = r XOR m for one m of 1 to 15, the same for all groups: groups come in pairs.
All inputs are finite; a program needn't handle non-finite values.
Results may differ from the reference program's by a relative error of at most 0.015.
Values may be sent and summed in bfloat16 or wider, within the bound.
No kernel may reach another device: no remote copies, remote signals or barrier semaphores. Data moves between devices by JAX's collectives and lax.ppermute only.
A program may use at most 128 MiB of HBM per device.

```python
import jax
import jax.numpy as jnp
from jax import lax

D = 8192
VOCAB = 128256
VDIM = 512
TOK_DEV = 512
TOKENS = 8192
N_REP = 16


def draw_token_ids(key, part):
    key = jax.random.fold_in(key, 11)
    first_key, second_key = jax.random.split(key)
    blocks = TOKENS // TOK_DEV
    position = jnp.arange(TOKENS, dtype=jnp.int32)
    block_index = position // TOK_DEV
    rolled = jax.random.randint(first_key, (N_REP, TOKENS), 0, 4 * (blocks - 1))
    live_mask = jnp.logical_or(rolled < blocks - 1 + 2 * block_index[None, :], (position % TOK_DEV == 0)[None, :])
    chosen = jax.random.randint(second_key, (N_REP, TOKENS), 1, VOCAB)
    return jnp.where(live_mask, chosen, 0).astype(jnp.int32)


def draw_matching(key, part):
    key = jax.random.fold_in(key, 23)
    flipper = jax.random.randint(key, (), 1, N_REP)
    return jnp.bitwise_xor(jnp.arange(N_REP, dtype=jnp.int32), flipper).astype(jnp.int32)


def raised(result, own_key, source, target, blocks, factor):
    def block_of(dim):
        return (jnp.arange(result.shape[dim]) // (result.shape[dim] // blocks)).reshape((-1,) + (1,) * (result.ndim - 1 - dim))

    near = jax.random.permutation(own_key, blocks)[block_of(target)]
    far = (block_of(target) + blocks // 2) % blocks
    return jnp.where((block_of(source) == near) | (block_of(source) == far), factor * result, result)


def block_scale(own_key, shape, pieces, low, high):
    level, own = 1.0, jax.random.fold_in(own_key, 6)
    for dim, blocks in pieces:
        steps = jnp.exp(jax.random.uniform(jax.random.fold_in(own, dim), (blocks,), jnp.float32, low / len(pieces), high / len(pieces)))
        level = level * jnp.repeat(steps, shape[dim] // blocks).reshape([-1 if axis == dim else 1 for axis in range(len(shape))])
    return level


def scatter_about(stream_key, extent, scale, reach, cuts=(), kind=jnp.bfloat16):
    entries = jax.random.normal(stream_key, extent, jnp.float32) * scale
    if len(cuts) > 0:
        entries = block_scale(stream_key, extent, cuts, -0.22, 0.18) * entries
    return jnp.clip(entries, min=-reach, max=reach).astype(kind)


def heavy_noise(own_key, shape, width, reach, cuts, heavy, kind=jnp.bfloat16):
    drawn = width * jax.random.normal(own_key, shape, jnp.float32)
    if cuts:
        drawn = drawn * block_scale(own_key, shape, cuts, -0.22, 0.18)
    return jnp.clip(raised(drawn, jax.random.fold_in(own_key, 3), *heavy), -reach, reach).astype(kind)


def setup_inputs(seed: int = 0) -> dict:
    key_of = jax.random.split(jax.random.key(seed), 6)
    hidden = heavy_noise(key_of[0], (N_REP, TOKENS, D), 1.0, 6.0, ((0, 16), (1, 16)), (1, 2, 16, 2.0))
    own_weight = scatter_about(key_of[1], (N_REP, D, VDIM), D ** -0.5, 0.0625, ((0, 16), (1, 16)))
    stale_weight = scatter_about(key_of[2], (N_REP, D, VDIM), D ** -0.5, 0.0625, ((0, 16), (1, 16)))
    token_ids = draw_token_ids(jax.random.fold_in(key_of[5], 71), 0)
    matching = draw_matching(jax.random.fold_in(key_of[5], 71), 0)
    return dict(hidden=hidden, own_weight=own_weight, stale_weight=stale_weight, token_ids=token_ids, matching=matching)


def group_gradient(packed):
    inputs, own_rows, partner_rows, id_rows = packed
    own_out = jnp.dot(inputs, own_rows, preferred_element_type=jnp.float32)
    partner_out = jnp.dot(inputs, partner_rows, preferred_element_type=jnp.float32)
    live_mask = (id_rows != 0).astype(jnp.float32)
    live_total = jnp.sum(live_mask)
    scaled_diff = ((own_out - partner_out) * (live_mask * lax.rsqrt(live_total))[:, None]).astype(jnp.bfloat16)
    blocks = TOKENS // TOK_DEV
    input_blocks = inputs.reshape(blocks, TOK_DEV, D)
    diff_blocks = scaled_diff.reshape(blocks, TOK_DEV, VDIM)

    def accumulate(running, pair):
        block_term = jnp.einsum('td,tw->dw', pair[0].astype(jnp.float32), pair[1].astype(jnp.float32))
        rounded = lax.optimization_barrier(block_term.astype(jnp.bfloat16))
        return (running + rounded.astype(jnp.float32), None)
    running, unused = lax.scan(accumulate, jnp.zeros((D, VDIM), jnp.float32), (input_blocks, diff_blocks))
    return running

def reference(hidden, own_weight, stale_weight, token_ids, matching):
    partner_weight = jnp.take(stale_weight, matching.astype(jnp.int32), axis=0)
    return lax.map(group_gradient, (hidden, own_weight, partner_weight, token_ids))
```

```python
import jax
import jax.numpy as jnp
from jax import lax
from jax.sharding import PartitionSpec as P

FAR = 2


def on_device(hidden, own_weight, stale_weight, token_ids, matching):
    features = hidden[0]
    own_rows = own_weight[0]
    n_rep, n_fsdp = lax.axis_size("rep"), lax.axis_size("fsdp")
    n_z = n_fsdp // FAR
    rows, columns = own_rows.shape
    first = columns // 2
    position = lax.axis_index("fsdp")
    z, far = position // FAR, position % FAR

    def up(shard):
        return lax.ppermute(shard, "fsdp", [(i, (i + FAR) % n_fsdp) for i in range(n_fsdp)])

    def down(shard):
        return lax.ppermute(shard, "fsdp", [(i, (i - FAR) % n_fsdp) for i in range(n_fsdp)])

    def across(shard):
        return lax.ppermute(shard, "fsdp", [(i, i ^ 1) for i in range(n_fsdp)])

    def hop(shard, distance):
        return lax.ppermute(shard, "fsdp", [(i, i ^ (FAR * distance)) for i in range(n_fsdp)])

    def swap(flip):
        return lambda shard: lax.ppermute(shard, "rep", [(i, i ^ flip) for i in range(n_rep)])

    fetched = lax.switch(matching[0] - 1, [swap(flip) for flip in range(1, n_rep)], stale_weight[0])
    delta = (own_rows.astype(jnp.float32) - fetched.astype(jnp.float32)).astype(jnp.bfloat16)
    mine_a, mine_b = delta[:, :first], delta[:, first:]

    live = (token_ids[0] != 0).astype(jnp.float32)

    def both_of(offset):
        at = ((z + offset) % n_z) * (FAR * rows)
        return lax.dynamic_slice_in_dim(features, at, FAR * rows, axis=1)

    def one_of(offset, side):
        at = (((z + offset) % n_z) * FAR + side) * rows
        return lax.dynamic_slice_in_dim(features, at, rows, axis=1)

    def times(left, right):
        return jnp.dot(left, right, preferred_element_type=jnp.float32)

    def transposed_times(left, right):
        return lax.dot_general(left, right, (((0,), (0,)), ((), ())), preferred_element_type=jnp.float32)

    half = n_z // 2

    got_b = {0: mine_b}
    for step in range(1, half + 1):
        if step < half:
            got_b[step] = None
    rising = falling = mine_b
    for step in range(1, half + 1):
        falling = down(falling)
        got_b[step] = falling
        if step < half:
            rising = up(rising)
            got_b[-step] = rising
    other_a = across(mine_a)
    pair_a = jnp.where(
        far == 0, jnp.concatenate([mine_a, other_a]), jnp.concatenate([other_a, mine_a])
    )
    got_a = {0: pair_a}
    rising = falling = pair_a
    for step in range(1, half + 1):
        rising = up(rising)
        got_a[-step] = rising
        if step < half:
            falling = down(falling)
            got_a[step] = falling
    groups = [[0]] + [[step, -step] for step in range(1, half)] + [[half]]
    other_b = {}
    for group in groups:
        sent = across(jnp.concatenate([got_b[o] for o in group]))
        for place, o in enumerate(group):
            other_b[o] = sent[place * rows : (place + 1) * rows]

    out_a = sum(times(both_of(o), got_a[o]) for o in got_a)
    out_b = sum(
        times(one_of(o, far), got_b[o]) + times(one_of(o, 1 - far), other_b[o])
        for group in groups
        for o in group
    )
    diff_a = (out_a * live[:, None]).astype(jnp.bfloat16)
    diff_b = (out_b * live[:, None]).astype(jnp.bfloat16)

    term_b = {}
    for group in reversed(groups):
        sent = across(
            jnp.concatenate(
                [transposed_times(one_of(o, 1 - far), diff_b).astype(jnp.bfloat16) for o in group]
            )
        )
        for place, o in enumerate(group):
            term_b[o] = (
                transposed_times(one_of(o, far), diff_b)
                + sent[place * rows : (place + 1) * rows].astype(jnp.float32)
            )
    falling = term_b[half].astype(jnp.bfloat16)
    rising = None
    for step in range(half - 1, -1, -1):
        falling = down(falling).astype(jnp.float32)
        if step > 0:
            falling = (falling + term_b[-step]).astype(jnp.bfloat16)
            if rising is None:
                rising = term_b[step].astype(jnp.bfloat16)
            else:
                rising = (up(rising).astype(jnp.float32) + term_b[step]).astype(jnp.bfloat16)
        else:
            rising = up(rising).astype(jnp.float32)
    total_b = term_b[0] + falling + rising

    def term_a(o):
        return transposed_times(both_of(o), diff_a)

    rising = term_a(half).astype(jnp.bfloat16)
    falling = None
    for step in range(half - 1, -1, -1):
        rising = up(rising).astype(jnp.float32)
        if step > 0:
            rising = (rising + term_a(step)).astype(jnp.bfloat16)
            if falling is None:
                falling = term_a(-step).astype(jnp.bfloat16)
            else:
                falling = (down(falling).astype(jnp.float32) + term_a(-step)).astype(jnp.bfloat16)
        else:
            falling = down(falling).astype(jnp.float32)
    sum_a = (term_a(0) + rising + falling).reshape(FAR, rows, first)
    leaving = lax.dynamic_index_in_dim(sum_a, 1 - far, keepdims=False).astype(jnp.bfloat16)
    total_a = lax.dynamic_index_in_dim(sum_a, far, keepdims=False) + across(leaving).astype(jnp.float32)

    count = jnp.full((8, 128), jnp.sum(live), jnp.float32)
    distance = 1
    while distance < n_z:
        count = count + hop(count, distance)
        distance *= 2
    count = count + across(count)
    gradient = jnp.concatenate([total_a, total_b], axis=1) * lax.rsqrt(count[0, 0])
    return gradient[None]


def solution(mesh):
    return jax.shard_map(
        on_device,
        mesh=mesh,
        in_specs=(
            P("rep", "fsdp", None),
            P("rep", "fsdp", None),
            P("rep", "fsdp", None),
            P("rep", "fsdp"),
            P(),
        ),
        out_specs=P("rep", "fsdp", None),
        check_vma=False,
    )
```

```python
import jax
import jax.numpy as jnp
from jax import lax
from jax.experimental import pallas as pl
from jax.experimental.pallas import tpu as pltpu
from jax.sharding import PartitionSpec as P

FAR = 2
NOTE = 16


def note_of(count, base):
    high = jnp.floor(count / base)
    top = lax.broadcasted_iota(jnp.int32, count.shape, 0) < NOTE // 2
    return jnp.where(top, high, count - base * high).astype(jnp.bfloat16)


def count_of(note, base):
    note = note.astype(jnp.float32)
    return jnp.broadcast_to(note[:1] * base + note[NOTE // 2 : NOTE // 2 + 1], note.shape)


class Sequence:
    def __init__(self, value):
        self.last = value

    def send(self, move, value):
        return move(lax.optimization_barrier((value, self.last))[0])

    def arrive(self, *values):
        values = lax.optimization_barrier((*values, self.last))[:-1]
        self.last = values[0]
        return values


SMALL = pl.CostEstimate(flops=1, bytes_accessed=1, transcendentals=0)
PARAMS = pltpu.CompilerParams(vmem_limit_bytes=24 * 2**20)
HERE = pl.BlockSpec(memory_space=pltpu.VMEM)
SCALARS = pl.BlockSpec(memory_space=pltpu.SMEM)


def park(features):
    def kernel(features_ref, out_ref, done):
        copy = pltpu.make_async_copy(features_ref, out_ref, done)
        copy.start()
        copy.wait()

    return pl.pallas_call(
        kernel,
        out_shape=jax.ShapeDtypeStruct(features.shape, features.dtype),
        in_specs=[pl.BlockSpec(memory_space=pl.ANY)],
        out_specs=HERE,
        scratch_shapes=[pltpu.SemaphoreType.DMA],
        compiler_params=PARAMS,
        cost_estimate=SMALL,
    )(features)


def split(own, stale, first):
    rows, columns = own.shape

    def kernel(own_ref, stale_ref, first_ref, second_ref):
        apart = (own_ref[...].astype(jnp.float32) - stale_ref[...].astype(jnp.float32)).T.astype(jnp.bfloat16)
        first_ref[...] = apart[:first]
        second_ref[...] = apart[first:]

    return pl.pallas_call(
        kernel,
        out_shape=[jax.ShapeDtypeStruct((n, rows), jnp.bfloat16) for n in (first, columns - first)],
        in_specs=[HERE, HERE],
        out_specs=[HERE, HERE],
        compiler_params=PARAMS,
        cost_estimate=SMALL,
    )(own, stale)


def forward(features, weights, plan, index, height, carry=None, live=None):
    tokens = features.shape[0]
    unit = tokens

    def kernel(index_ref, features_ref, *refs):
        refs = list(refs)
        total, out_ref = refs.pop(), refs.pop()
        total[...] = jnp.zeros_like(total) if carry is None else refs.pop()[...]
        if live is not None:
            live_ref = refs.pop()
        for which, source, target, slot, width in plan:
            at = pl.multiple_of(index_ref[slot] * unit, unit)
            total[target, :] += lax.dot_general(
                refs[which][source, :],
                features_ref[:, pl.ds(at, width)],
                (((1,), (1,)), ((), ())),
                preferred_element_type=jnp.float32,
            )
        out_ref[...] = total[...] if live is None else (total[...] * live_ref[...]).astype(jnp.bfloat16)

    extra = ([] if live is None else [live]) + ([] if carry is None else [carry])
    return pl.pallas_call(
        kernel,
        out_shape=jax.ShapeDtypeStruct((height, tokens), jnp.float32 if live is None else jnp.bfloat16),
        in_specs=[SCALARS] + [HERE] * (1 + len(weights) + len(extra)),
        out_specs=HERE,
        scratch_shapes=[pltpu.VMEM((height, tokens), jnp.float32)],
        compiler_params=PARAMS,
        cost_estimate=SMALL,
    )(index, features, *weights, *extra)


def backward(diff, features, index, slots, width, dtype):
    unit = features.shape[0]
    n, height = len(slots), diff.shape[0]

    def kernel(index_ref, diff_ref, features_ref, out_ref):
        for place, slot in enumerate(slots):
            at = pl.multiple_of(index_ref[slot] * unit, unit)
            block = features_ref[:, pl.ds(at, width)]
            out_ref[place] = jnp.dot(diff_ref[...], block, preferred_element_type=jnp.float32).astype(dtype)

    return pl.pallas_call(
        kernel,
        out_shape=jax.ShapeDtypeStruct((n, height, width), dtype),
        in_specs=[SCALARS, HERE, HERE],
        out_specs=HERE,
        compiler_params=PARAMS,
        cost_estimate=SMALL,
    )(index, diff, features)


def on_device(hidden, own_weight, stale_weight, token_ids, matching):
    own_rows = own_weight[0]
    n_rep, n_fsdp = lax.axis_size("rep"), lax.axis_size("fsdp")
    n_z = n_fsdp // FAR
    half = n_z // 2
    rows, columns = own_rows.shape
    first = columns * 3 // 8
    second = columns - first
    middle = second // 2
    both = FAR * rows
    position = lax.axis_index("fsdp")
    z, far = position // FAR, position % FAR

    def up(shard):
        return lax.ppermute(shard, "fsdp", [(i, (i + FAR) % n_fsdp) for i in range(n_fsdp)])

    def down(shard):
        return lax.ppermute(shard, "fsdp", [(i, (i - FAR) % n_fsdp) for i in range(n_fsdp)])

    def across(shard):
        return lax.ppermute(shard, "fsdp", [(i, i ^ 1) for i in range(n_fsdp)])

    def swap(flip):
        return lambda shard: lax.ppermute(shard, "rep", [(i, i ^ flip) for i in range(n_rep)])

    fetched = lax.switch(matching[0] - 1, [swap(flip) for flip in range(1, n_rep)], stale_weight[0])
    mine_a, mine_b = split(own_rows, fetched, first)
    line = Sequence(mine_b)
    ids = lax.optimization_barrier((token_ids[0], fetched))[0]
    live = (ids != 0).astype(jnp.float32)[None]
    marks = jnp.broadcast_to(live.astype(jnp.bfloat16), (NOTE, rows))
    note = note_of(
        jnp.dot(marks, jnp.ones((rows, both), jnp.bfloat16), preferred_element_type=jnp.float32), 128
    )

    order = [0, 1, -1, 2, -2, 3, -3, 4]
    back = [4, 3, -3, 2, -2, 1, -1, 0]
    near_side, far_side = len(order) * FAR, len(order) * FAR * 2
    offsets = jnp.asarray([o for o in order for _ in range(FAR)] * 3, jnp.int32)
    place = lax.iota(jnp.int32, len(order) * FAR * 3)
    side = jnp.where(place < near_side, place % FAR, jnp.where(place < far_side, far, 1 - far))
    index = (z + offsets) % n_z * FAR + side

    def slot_a(o, side=0):
        return order.index(o) * FAR + side

    def slot_near(o):
        return near_side + order.index(o) * FAR

    def slot_far(o):
        return far_side + order.index(o) * FAR

    def send_pair(rising, falling):
        return line.send(up, rising), line.send(down, falling)

    a, b, x = {}, {0: mine_b}, {}

    def cross(*group):
        return line.send(across, jnp.concatenate([b[o] for o in group]))

    def crossed(sent, *group):
        for at, o in enumerate(group):
            x[o] = sent[at * second : (at + 1) * second]

    xa = line.send(across, mine_a)
    b1 = send_pair(b[0], b[0])
    features = park(lax.optimization_barrier((hidden[0], line.last))[0])
    xa, features = line.arrive(xa, features)
    pair_a = jnp.concatenate([jnp.where(far == 0, mine_a, xa), jnp.where(far == 0, xa, mine_a)], axis=1)
    a[0] = jnp.concatenate([pair_a, note])
    a1 = send_pair(a[0], a[0])
    x0 = cross(0)
    b[-1], b[1] = line.arrive(*b1)
    b2 = send_pair(b[-1], b[1])
    x1 = cross(1, -1)
    a[-1], a[1], x0 = line.arrive(*a1, x0)
    a2 = send_pair(a[-1], a[1])
    b[-2], b[2] = line.arrive(*b2)
    b3 = send_pair(b[-2], b[2])
    x2 = cross(2, -2)
    a[-2], a[2], x1 = line.arrive(*a2, x1)
    a3 = send_pair(a[-2], a[2])
    b[-3], b[3] = line.arrive(*b3)
    b4 = send_pair(b[-3][:middle], b[3][middle:])
    x3 = cross(3, -3)
    side, all_b = slice(0, first), slice(0, second)
    near = [a[o] for o in order[:5]]
    near[0], mark = lax.optimization_barrier((near[0], line.last))
    plan = [(at, side, side, slot_a(order[at]), both) for at in range(5)]
    part_a = forward(features, near, plan, index, first)
    a[-3], a[3], x2, part_a = line.arrive(*a3, x2, part_a)
    a4 = send_pair(a[-3][:first, :rows], a[3][:, rows:])
    low_b, high_b = line.arrive(*b4)
    b[4] = jnp.concatenate([low_b, high_b])
    x4 = cross(4)
    near = [b[o] for o in order[:7]] + [x0, x1, x2]
    near[0], mark = lax.optimization_barrier((near[0], line.last))

    def stacked(which, place, slot):
        return (which, slice(place * second, (place + 1) * second), all_b, slot, rows)

    plan = [stacked(at, 0, slot_near(order[at])) for at in range(7)] + [stacked(7, 0, slot_far(0))]
    plan += [stacked(7 + step, place, slot_far((step, -step)[place])) for step in (1, 2) for place in range(2)]
    part_b = forward(features, near, plan, index, second)
    low_a, high_a, x3, part_b = line.arrive(*a4, x3, part_b)
    high = high_a
    counts = [count_of(a[o][first:], 128)[:, :rows] for o in range(-3, 4)] + [count_of(high[first:], 128)]

    plan = [(0, side, side, slot_a(3), both), (1, side, side, slot_a(-3), both)]
    plan += [(2, side, side, slot_a(4), rows), (3, side, side, slot_a(4, 1), rows)]
    diff_a = forward(features, [a[3], a[-3], low_a, high_a], plan, index, first, part_a, live)

    def add(arrived, term):
        return (arrived.astype(jnp.float32) + term).astype(jnp.bfloat16)

    start = backward(diff_a, features, index, [slot_a(4), slot_a(4, 1)], rows, jnp.bfloat16)
    a1 = send_pair(start[0], start[1])
    (x4,) = line.arrive(x4)
    top, bottom = slice(0, middle), slice(middle, second)
    plan = [(0, top, top, slot_near(4), rows), (1, top, bottom, slot_near(4), rows)]
    plan += [stacked(2, 0, slot_far(3)), stacked(2, 1, slot_far(-3)), stacked(3, 0, slot_far(4))]
    diff_b = forward(features, [low_b, high_b, x3, x4], plan, index, second, part_b, live)
    away = backward(diff_b, features, index, [slot_far(o) for o in back[:3]], rows, jnp.bfloat16)
    x0 = line.send(across, away[0])
    x1 = line.send(across, away[1:].reshape(-1, rows))
    rest = backward(diff_a, features, index, [slot_a(o) for o in back[1:]], both, jnp.float32)
    term_a = {o: rest[at] for at, o in enumerate([3, -3, 2, -2, 1, -1, 0])}
    keep = backward(diff_b, features, index, [slot_near(o) for o in back], rows, jnp.float32)
    away = backward(diff_b, features, index, [slot_far(o) for o in back[3:]], rows, jnp.bfloat16)
    term = {}

    def cross_back(*group):
        at = back.index(group[0]) - 3
        return line.send(across, away[at : at + len(group)].reshape(-1, rows))

    def crossed_back(sent, *group):
        for at, o in enumerate(group):
            part = sent[at * second : (at + 1) * second].astype(jnp.float32)
            term[o] = keep[back.index(o)] + part

    rising, falling, away, keep, rest = line.arrive(*a1, away, keep, rest)
    term_a = {o: rest[at] for at, o in enumerate([3, -3, 2, -2, 1, -1, 0])}
    above, below = term_a[3], term_a[-3]
    above = jnp.concatenate([add(rising, above[:, :rows]), above[:, rows:].astype(jnp.bfloat16)], axis=1)
    below = jnp.concatenate([below[:, :rows].astype(jnp.bfloat16), add(falling, below[:, rows:])], axis=1)
    a2 = send_pair(above, below)
    (x0,) = line.arrive(x0)
    crossed_back(x0, 4)
    start = term[4].astype(jnp.bfloat16)
    b1 = send_pair(start[:middle], start[middle:])
    x2 = cross_back(2, -2)
    rising, falling = line.arrive(*a2)
    a3 = send_pair(add(rising, term_a[2]), add(falling, term_a[-2]))
    rising, falling, x1 = line.arrive(*b1, x1)
    crossed_back(x1, 3, -3)
    above = jnp.concatenate([add(rising, term[3][:middle]), term[3][middle:].astype(jnp.bfloat16)])
    below = jnp.concatenate([term[-3][:middle].astype(jnp.bfloat16), add(falling, term[-3][middle:])])
    b2 = send_pair(above, below)
    x3 = cross_back(1, -1)
    rising, falling = line.arrive(*a3)
    a4 = send_pair(add(rising, term_a[1]), add(falling, term_a[-1]))
    rising, falling, x2 = line.arrive(*b2, x2)
    crossed_back(x2, 2, -2)
    b3 = send_pair(add(rising, term[2]), add(falling, term[-2]))
    x4 = cross_back(0)
    rising, falling = line.arrive(*a4)
    sum_a = term_a[0] + rising.astype(jnp.float32) + falling.astype(jnp.float32)
    leaving = lax.dynamic_slice_in_dim(sum_a, (1 - far) * rows, rows, axis=1).astype(jnp.bfloat16)
    live_z = sum(counts)
    xa = line.send(across, jnp.concatenate([leaving, note_of(live_z, 64)]))
    rising, falling, x3 = line.arrive(*b3, x3)
    crossed_back(x3, 1, -1)
    b4 = send_pair(add(rising, term[1]), add(falling, term[-1]))
    x4, xa = line.arrive(x4, xa)
    crossed_back(x4, 0)
    rising, falling = line.arrive(*b4)
    total_b = term[0] + rising.astype(jnp.float32) + falling.astype(jnp.float32)
    total_a = lax.dynamic_slice_in_dim(sum_a, far * rows, rows, axis=1) + xa[:first].astype(jnp.float32)
    scale = lax.rsqrt(live_z + count_of(xa[first:], 64))[:1]

    return (jnp.concatenate([total_a, total_b]) * scale).T[None]


def solution(mesh):
    return jax.shard_map(
        on_device,
        mesh=mesh,
        in_specs=(
            P("rep", "fsdp", None),
            P("rep", "fsdp", None),
            P("rep", "fsdp", None),
            P("rep", "fsdp"),
            P(),
        ),
        out_specs=P("rep", "fsdp", None),
        check_vma=False,
    )
```

```python
import jax
import jax.numpy as jnp
from jax import lax
from jax.experimental import pallas as pl
from jax.experimental.pallas import tpu as pltpu
from jax.sharding import PartitionSpec as P

FAR = 2
NOTE = 16


def note_of(count, base):
    high = jnp.floor(count / base)
    top = lax.broadcasted_iota(jnp.int32, count.shape, 0) < NOTE // 2
    return jnp.where(top, high, count - base * high).astype(jnp.bfloat16)


def count_of(note, base):
    note = note.astype(jnp.float32)
    return jnp.broadcast_to(note[:1] * base + note[NOTE // 2 : NOTE // 2 + 1], note.shape)


class Sequence:
    def __init__(self, value):
        self.last = value

    def send(self, move, value):
        return move(lax.optimization_barrier((value, self.last))[0])

    def arrive(self, *values):
        values = lax.optimization_barrier((*values, self.last))[:-1]
        self.last = values[0]
        return values


SMALL = pl.CostEstimate(flops=1, bytes_accessed=1, transcendentals=0)
PARAMS = pltpu.CompilerParams(vmem_limit_bytes=24 * 2**20)
HERE = pl.BlockSpec(memory_space=pltpu.VMEM)
SCALARS = pl.BlockSpec(memory_space=pltpu.SMEM)


def park(features):
    def kernel(features_ref, out_ref, done):
        copy = pltpu.make_async_copy(features_ref, out_ref, done)
        copy.start()
        copy.wait()

    return pl.pallas_call(
        kernel,
        out_shape=jax.ShapeDtypeStruct(features.shape, features.dtype),
        in_specs=[pl.BlockSpec(memory_space=pl.ANY)],
        out_specs=HERE,
        scratch_shapes=[pltpu.SemaphoreType.DMA],
        compiler_params=PARAMS,
        cost_estimate=SMALL,
    )(features)


def split(own, stale, first):
    rows, columns = own.shape

    def kernel(own_ref, stale_ref, first_ref, second_ref):
        apart = (own_ref[...].astype(jnp.float32) - stale_ref[...].astype(jnp.float32)).T.astype(jnp.bfloat16)
        first_ref[...] = apart[:first]
        second_ref[...] = apart[first:]

    return pl.pallas_call(
        kernel,
        out_shape=[jax.ShapeDtypeStruct((n, rows), jnp.bfloat16) for n in (first, columns - first)],
        in_specs=[HERE, HERE],
        out_specs=[HERE, HERE],
        compiler_params=PARAMS,
        cost_estimate=SMALL,
    )(own, stale)


def forward(features, weights, plan, index, height, carry=None, live=None):
    tokens = features.shape[0]
    unit = tokens

    def kernel(index_ref, features_ref, *refs):
        refs = list(refs)
        total, out_ref = refs.pop(), refs.pop()
        total[...] = jnp.zeros_like(total) if carry is None else refs.pop()[...]
        if live is not None:
            live_ref = refs.pop()
        for which, source, target, slot, width in plan:
            at = pl.multiple_of(index_ref[slot] * unit, unit)
            total[target, :] += lax.dot_general(
                refs[which][source, :],
                features_ref[:, pl.ds(at, width)],
                (((1,), (1,)), ((), ())),
                preferred_element_type=jnp.float32,
            )
        out_ref[...] = total[...] if live is None else (total[...] * live_ref[...]).astype(jnp.bfloat16)

    extra = ([] if live is None else [live]) + ([] if carry is None else [carry])
    return pl.pallas_call(
        kernel,
        out_shape=jax.ShapeDtypeStruct((height, tokens), jnp.float32 if live is None else jnp.bfloat16),
        in_specs=[SCALARS] + [HERE] * (1 + len(weights) + len(extra)),
        out_specs=HERE,
        scratch_shapes=[pltpu.VMEM((height, tokens), jnp.float32)],
        compiler_params=PARAMS,
        cost_estimate=SMALL,
    )(index, features, *weights, *extra)


def backward(diff, features, index, slots, width, dtype):
    unit = features.shape[0]
    n, height = len(slots), diff.shape[0]

    def kernel(index_ref, diff_ref, features_ref, out_ref):
        for place, slot in enumerate(slots):
            at = pl.multiple_of(index_ref[slot] * unit, unit)
            block = features_ref[:, pl.ds(at, width)]
            out_ref[place] = jnp.dot(diff_ref[...], block, preferred_element_type=jnp.float32).astype(dtype)

    return pl.pallas_call(
        kernel,
        out_shape=jax.ShapeDtypeStruct((n, height, width), dtype),
        in_specs=[SCALARS, HERE, HERE],
        out_specs=HERE,
        compiler_params=PARAMS,
        cost_estimate=SMALL,
    )(index, diff, features)


def on_device(hidden, own_weight, stale_weight, token_ids, matching):
    own_rows = own_weight[0]
    n_rep, n_fsdp = lax.axis_size("rep"), lax.axis_size("fsdp")
    n_z = n_fsdp // FAR
    half = n_z // 2
    rows, columns = own_rows.shape
    first = columns * 3 // 8
    second = columns - first
    middle = second // 2
    both = FAR * rows
    position = lax.axis_index("fsdp")
    z, far = position // FAR, position % FAR

    def up(shard):
        return lax.ppermute(shard, "fsdp", [(i, (i + FAR) % n_fsdp) for i in range(n_fsdp)])

    def down(shard):
        return lax.ppermute(shard, "fsdp", [(i, (i - FAR) % n_fsdp) for i in range(n_fsdp)])

    def across(shard):
        return lax.ppermute(shard, "fsdp", [(i, i ^ 1) for i in range(n_fsdp)])

    def swap(flip):
        return lambda shard: lax.ppermute(shard, "rep", [(i, i ^ flip) for i in range(n_rep)])

    fetched = lax.switch(matching[0] - 1, [swap(flip) for flip in range(1, n_rep)], stale_weight[0])
    mine_a, mine_b = split(own_rows, fetched, first)
    line = Sequence(mine_b)
    ids = lax.optimization_barrier((token_ids[0], fetched))[0]
    live = (ids != 0).astype(jnp.float32)[None]
    marks = jnp.broadcast_to(live.astype(jnp.bfloat16), (NOTE, rows))
    note = note_of(
        jnp.dot(marks, jnp.ones((rows, both), jnp.bfloat16), preferred_element_type=jnp.float32), 128
    )

    order = [0, 1, -1, 2, -2, 3, -3, 4]
    back = [4, 3, -3, 2, -2, 1, -1, 0]
    near_side, far_side = len(order) * FAR, len(order) * FAR * 2
    offsets = jnp.asarray([o for o in order for _ in range(FAR)] * 3, jnp.int32)
    place = lax.iota(jnp.int32, len(order) * FAR * 3)
    side = jnp.where(place < near_side, place % FAR, jnp.where(place < far_side, far, 1 - far))
    index = (z + offsets) % n_z * FAR + side

    def slot_a(o, side=0):
        return order.index(o) * FAR + side

    def slot_near(o):
        return near_side + order.index(o) * FAR

    def slot_far(o):
        return far_side + order.index(o) * FAR

    def send_pair(rising, falling):
        return line.send(up, rising), line.send(down, falling)

    a, b, x = {}, {0: mine_b}, {}

    def cross(*group):
        return line.send(across, jnp.concatenate([b[o] for o in group]))

    def crossed(sent, *group):
        for at, o in enumerate(group):
            x[o] = sent[at * second : (at + 1) * second]

    xa = line.send(across, mine_a)
    b1 = send_pair(b[0], b[0])
    (xa,) = line.arrive(xa)
    pair_a = jnp.concatenate([jnp.where(far == 0, mine_a, xa), jnp.where(far == 0, xa, mine_a)], axis=1)
    a[0] = jnp.concatenate([pair_a, note])
    a1 = send_pair(a[0], a[0])
    x0 = cross(0)
    b[-1], b[1] = line.arrive(*b1)
    b2 = send_pair(b[-1], b[1])
    x1 = cross(1, -1)
    a[-1], a[1], x0 = line.arrive(*a1, x0)
    a2 = send_pair(a[-1], a[1])
    b[-2], b[2] = line.arrive(*b2)
    b3 = send_pair(b[-2], b[2])
    x2 = cross(2, -2)
    a[-2], a[2], x1 = line.arrive(*a2, x1)
    a3 = send_pair(a[-2], a[2])
    b[-3], b[3] = line.arrive(*b3)
    b4 = send_pair(b[-3][:middle], b[3][middle:])
    x3 = cross(3, -3)
    side, all_b = slice(0, first), slice(0, second)
    near = [a[o] for o in order[:5]]
    near[0], mark = lax.optimization_barrier((near[0], line.last))
    plan = [(at, side, side, slot_a(order[at]), both) for at in range(5)]
    features = park(lax.optimization_barrier((hidden[0], line.last))[0])
    part_a = forward(features, near, plan, index, first)
    a[-3], a[3], x2, part_a = line.arrive(*a3, x2, part_a)
    a4 = send_pair(a[-3][:first, :rows], a[3][:, rows:])
    low_b, high_b = line.arrive(*b4)
    b[4] = jnp.concatenate([low_b, high_b])
    x4 = cross(4)
    near = [b[o] for o in order[:7]] + [x0, x1, x2]
    near[0], mark = lax.optimization_barrier((near[0], line.last))

    def stacked(which, place, slot):
        return (which, slice(place * second, (place + 1) * second), all_b, slot, rows)

    plan = [stacked(at, 0, slot_near(order[at])) for at in range(7)] + [stacked(7, 0, slot_far(0))]
    plan += [stacked(7 + step, place, slot_far((step, -step)[place])) for step in (1, 2) for place in range(2)]
    part_b = forward(features, near, plan, index, second)
    low_a, high_a, x3, part_b = line.arrive(*a4, x3, part_b)
    high = high_a
    counts = [count_of(a[o][first:], 128)[:, :rows] for o in range(-3, 4)] + [count_of(high[first:], 128)]

    plan = [(0, side, side, slot_a(3), both), (1, side, side, slot_a(-3), both)]
    plan += [(2, side, side, slot_a(4), rows), (3, side, side, slot_a(4, 1), rows)]
    diff_a = forward(features, [a[3], a[-3], low_a, high_a], plan, index, first, part_a, live)

    def add(arrived, term):
        return (arrived.astype(jnp.float32) + term).astype(jnp.bfloat16)

    start = backward(diff_a, features, index, [slot_a(4), slot_a(4, 1)], rows, jnp.bfloat16)
    a1 = send_pair(start[0], start[1])
    (x4,) = line.arrive(x4)
    top, bottom = slice(0, middle), slice(middle, second)
    plan = [(0, top, top, slot_near(4), rows), (1, top, bottom, slot_near(4), rows)]
    plan += [stacked(2, 0, slot_far(3)), stacked(2, 1, slot_far(-3)), stacked(3, 0, slot_far(4))]
    diff_b = forward(features, [low_b, high_b, x3, x4], plan, index, second, part_b, live)
    away = backward(diff_b, features, index, [slot_far(o) for o in back[:3]], rows, jnp.bfloat16)
    x0 = line.send(across, away[0])
    x1 = line.send(across, away[1:].reshape(-1, rows))
    rest = backward(diff_a, features, index, [slot_a(o) for o in back[1:]], both, jnp.float32)
    term_a = {o: rest[at] for at, o in enumerate([3, -3, 2, -2, 1, -1, 0])}
    keep = backward(diff_b, features, index, [slot_near(o) for o in back], rows, jnp.float32)
    away = backward(diff_b, features, index, [slot_far(o) for o in back[3:]], rows, jnp.bfloat16)
    term = {}

    def cross_back(*group):
        at = back.index(group[0]) - 3
        return line.send(across, away[at : at + len(group)].reshape(-1, rows))

    def crossed_back(sent, *group):
        for at, o in enumerate(group):
            part = sent[at * second : (at + 1) * second].astype(jnp.float32)
            term[o] = keep[back.index(o)] + part

    rising, falling, away, keep, rest = line.arrive(*a1, away, keep, rest)
    term_a = {o: rest[at] for at, o in enumerate([3, -3, 2, -2, 1, -1, 0])}
    above, below = term_a[3], term_a[-3]
    above = jnp.concatenate([add(rising, above[:, :rows]), above[:, rows:].astype(jnp.bfloat16)], axis=1)
    below = jnp.concatenate([below[:, :rows].astype(jnp.bfloat16), add(falling, below[:, rows:])], axis=1)
    a2 = send_pair(above, below)
    (x0,) = line.arrive(x0)
    crossed_back(x0, 4)
    start = term[4].astype(jnp.bfloat16)
    b1 = send_pair(start[:middle], start[middle:])
    x2 = cross_back(2, -2)
    rising, falling = line.arrive(*a2)
    a3 = send_pair(add(rising, term_a[2]), add(falling, term_a[-2]))
    rising, falling, x1 = line.arrive(*b1, x1)
    crossed_back(x1, 3, -3)
    above = jnp.concatenate([add(rising, term[3][:middle]), term[3][middle:].astype(jnp.bfloat16)])
    below = jnp.concatenate([term[-3][:middle].astype(jnp.bfloat16), add(falling, term[-3][middle:])])
    b2 = send_pair(above, below)
    x3 = cross_back(1, -1)
    rising, falling = line.arrive(*a3)
    a4 = send_pair(add(rising, term_a[1]), add(falling, term_a[-1]))
    rising, falling, x2 = line.arrive(*b2, x2)
    crossed_back(x2, 2, -2)
    b3 = send_pair(add(rising, term[2]), add(falling, term[-2]))
    x4 = cross_back(0)
    rising, falling = line.arrive(*a4)
    sum_a = term_a[0] + rising.astype(jnp.float32) + falling.astype(jnp.float32)
    leaving = lax.dynamic_slice_in_dim(sum_a, (1 - far) * rows, rows, axis=1).astype(jnp.bfloat16)
    live_z = sum(counts)
    xa = line.send(across, jnp.concatenate([leaving, note_of(live_z, 64)]))
    rising, falling, x3 = line.arrive(*b3, x3)
    crossed_back(x3, 1, -1)
    b4 = send_pair(add(rising, term[1]), add(falling, term[-1]))
    x4, xa = line.arrive(x4, xa)
    crossed_back(x4, 0)
    rising, falling = line.arrive(*b4)
    total_b = term[0] + rising.astype(jnp.float32) + falling.astype(jnp.float32)
    total_a = lax.dynamic_slice_in_dim(sum_a, far * rows, rows, axis=1) + xa[:first].astype(jnp.float32)
    scale = lax.rsqrt(live_z + count_of(xa[first:], 64))[:1]

    return (jnp.concatenate([total_a, total_b]) * scale).T[None]


def solution(mesh):
    return jax.shard_map(
        on_device,
        mesh=mesh,
        in_specs=(
            P("rep", "fsdp", None),
            P("rep", "fsdp", None),
            P("rep", "fsdp", None),
            P("rep", "fsdp"),
            P(),
        ),
        out_specs=P("rep", "fsdp", None),
        check_vma=False,
    )
```
